32 devices in a mesh: grp: 1, seq: 32 (over z, y, x, core).
Axes of the slice: x: 2, y: 2, z: 4, core: 2. Of those that a mesh axis runs over, the one named last changes fastest.
Arguments:
- tokens: bfloat16 [4096, 4096], P(('grp', 'seq')), may hold values from -6 to 6
- gain: float32 [4096], replicated, may hold values from 0.5 to 6, as said below
- w_query: bfloat16 [4096, 2048], P('seq'), may hold values from -0.09375 to 0.09375
- key_value_weight: bfloat16 [4096, 1024], P('seq'), may hold values from -0.09375 to 0.09375
Outputs:
- attended: bfloat16 [4096, 2048], P(('grp', 'seq'))
The draws below stay inside these ranges and needn't reach their ends.
Inputs may be any that keep to these rules, and one draw needn't show every extreme that they name: gain is the same for all groups.
All inputs are finite; a program needn't handle non-finite values.
Results may differ from the reference program's by a relative error of at most 0.0055.
The reference program's roundings to bfloat16 on the way count: a program that leaves them out, or rounds other values in their place, can miss the bound.
Values may be sent and summed in bfloat16 or wider, within the bound.
A program may use at most 128 MiB of HBM per device.

```python
import jax
import jax.numpy as jnp
from jax import lax

MODEL_WIDTH = 4096
HEAD_WIDTH = 128
HQ = 16
KEY_VALUE_HEADS = 4
QUERY_PER_KEY = 4
LOCAL_TOKENS = 128
SEQUENCE_TOKENS = 4096


def draw_gain(key, part):
    return jax.random.uniform(key, (MODEL_WIDTH,), jnp.float32, 0.5, 1.5)


def levels(rng, dims, split, smallest, high):
    factor_of, own = 1.0, jax.random.fold_in(rng, 6)
    for position, blocks in split:
        steps = jnp.exp(jax.random.uniform(jax.random.fold_in(own, position), (blocks,), jnp.float32, smallest / len(split), high / len(split)))
        factor_of = factor_of * jnp.repeat(steps, dims[position] // blocks).reshape([-1 if axis == position else 1 for axis in range(len(dims))])
    return factor_of


def noise(rng, extent, deviation, most, split=(), held_as=jnp.bfloat16):
    array = jax.random.normal(rng, extent, jnp.float32) * deviation
    if len(split) > 0:
        array = levels(rng, extent, split, -0.22, 0.18) * array
    return jnp.clip(array, min=-most, max=most).astype(held_as)


def setup_inputs(seed: int = 0, part: int = 0) -> dict:
    arg_keys = jax.random.split(jax.random.key(seed), 5)
    part_splits = jax.random.split(jax.random.fold_in(arg_keys[4], part), 5)
    tokens = noise(part_splits[0], (SEQUENCE_TOKENS, MODEL_WIDTH), 1.0, 6.0, ((0, 32),))
    gain = draw_gain(jax.random.fold_in(arg_keys[4], 71), part)
    w_query = noise(arg_keys[2], (MODEL_WIDTH, HQ * HEAD_WIDTH), MODEL_WIDTH ** -0.5, 0.09375, ((0, 32),))
    key_value_weight = noise(arg_keys[3], (MODEL_WIDTH, 2 * KEY_VALUE_HEADS * HEAD_WIDTH), MODEL_WIDTH ** -0.5, 0.09375, ((0, 32),))
    return dict(tokens=tokens, gain=gain, w_query=w_query, key_value_weight=key_value_weight)


ROPE_BASE = 500000.0

def apply_rotation(heads_in, token_positions):
    half_dim = HEAD_WIDTH // 2
    frequency = ROPE_BASE ** (-(jnp.arange(half_dim, dtype=jnp.float32) * 2.0 / HEAD_WIDTH))
    angles = token_positions.astype(jnp.float32)[:, None] * frequency[None, :]
    cosine = jnp.cos(angles)[:, None, :]
    sine_part = jnp.sin(angles)[:, None, :]
    first = heads_in[..., :half_dim]
    second = heads_in[..., half_dim:]
    return jnp.concatenate([first * cosine - second * sine_part, second * cosine + first * sine_part], axis=-1)

def reference(tokens, gain, w_query, key_value_weight):
    tok_float = tokens.astype(jnp.float32)
    mean_sq = lax.optimization_barrier(jnp.mean(tok_float * tok_float, axis=-1, keepdims=True))
    normed = (tok_float * lax.rsqrt(mean_sq + 1e-05) * gain[None, :]).astype(jnp.bfloat16)
    query_raw = jnp.dot(normed, w_query, preferred_element_type=jnp.float32)
    key_value_rows = jnp.dot(normed, key_value_weight, preferred_element_type=jnp.float32)
    token_positions = jnp.arange(SEQUENCE_TOKENS, dtype=jnp.int32)
    query_matrix = apply_rotation(query_raw.reshape(SEQUENCE_TOKENS, HQ, HEAD_WIDTH), token_positions).astype(jnp.bfloat16)
    query_matrix = query_matrix.reshape(SEQUENCE_TOKENS // LOCAL_TOKENS, LOCAL_TOKENS, KEY_VALUE_HEADS, QUERY_PER_KEY, HEAD_WIDTH)
    key_head_rows = apply_rotation(key_value_rows[:, :KEY_VALUE_HEADS * HEAD_WIDTH].reshape(SEQUENCE_TOKENS, KEY_VALUE_HEADS, HEAD_WIDTH), token_positions).astype(jnp.bfloat16)
    value_head_rows = key_value_rows[:, KEY_VALUE_HEADS * HEAD_WIDTH:].reshape(SEQUENCE_TOKENS, KEY_VALUE_HEADS, HEAD_WIDTH).astype(jnp.bfloat16)
    key_float = key_head_rows.astype(jnp.float32)
    value_float = value_head_rows.astype(jnp.float32)
    scale = 1.0 / HEAD_WIDTH ** 0.5
    starts = (jnp.arange(SEQUENCE_TOKENS // LOCAL_TOKENS, dtype=jnp.int32) * LOCAL_TOKENS).astype(jnp.int32)

    def one_block(inputs):
        query_block, first_row = inputs
        scores = jnp.einsum('qhgd,khd->qhgk', query_block.astype(jnp.float32), key_float) * scale
        query_pos = first_row + jnp.arange(LOCAL_TOKENS, dtype=jnp.int32)
        allowed = jnp.arange(SEQUENCE_TOKENS, dtype=jnp.int32)[None, :] <= query_pos[:, None]
        scores = jnp.where(allowed[:, None, None, :], scores, -1e+30)
        row_max = lax.optimization_barrier(jnp.max(scores, axis=-1, keepdims=True))
        expo = jnp.exp(scores - row_max)
        totals = lax.optimization_barrier(jnp.sum(expo, axis=-1))
        probs = expo.astype(jnp.bfloat16).astype(jnp.float32)
        weighted = jnp.einsum('qhgk,khd->qhgd', probs, value_float)
        result = weighted / totals[..., None]
        return result.reshape(LOCAL_TOKENS, HQ * HEAD_WIDTH).astype(jnp.bfloat16)
    attended = lax.map(one_block, (query_matrix, starts))
    return attended.reshape(SEQUENCE_TOKENS, HQ * HEAD_WIDTH)
```

```python
import functools

import jax
import jax.numpy as jnp
from jax import lax
from jax.experimental import pallas as pl
from jax.experimental.pallas import tpu as pltpu
from jax.sharding import PartitionSpec as P

HEAD_WIDTH = 128
HQ = 16
ROPE_BASE = 500000.0
LOG2E = 1.4426950408889634
MESH = pl.DeviceIdType.MESH


def kernel(
    planes, kv_heads, tok_ref, gain_ref, wq_ref, wkv_ref, cos_ref, sin_ref, out_ref,
    wst, wbuf, xbuf, acc, qbuf, kvbuf, mbuf, lbuf, obuf, ost, orecv,
    ws, wr, xs, xr, us, ur, ds_, dr, ss, sr, ks, kr, kss, ksr, os_, orr,
):
    C, Z, D = kv_heads, planes, HEAD_WIDTH
    T, M = tok_ref.shape
    G = HQ // C
    QW = G * D
    R = C * T
    me = lax.axis_index("seq")
    z = me // (2 * C)
    p = (me % (2 * C)) // 2
    k = me % 2

    def dev(zi, pi, ki):
        return {"seq": (zi * C + pi) * 2 + ki}

    sibling = dev(z, p, 1 - k)
    above = dev(lax.rem(z + 1, Z), p, k)
    below = dev(lax.rem(z + Z - 1, Z), p, k)
    has_above = z < Z - 1
    has_below = z > 0

    def copy(src, dst, send, recv, device):
        return pltpu.make_async_remote_copy(
            src_ref=src, dst_ref=dst, send_sem=send, recv_sem=recv,
            device_id=device, device_id_type=MESH,
        )

    barrier = pltpu.get_barrier_semaphore()
    for d in range(1, C):
        pl.semaphore_signal(barrier, inc=1, device_id=dev(z, lax.rem(p + d, C), k), device_id_type=MESH)
    pl.semaphore_signal(barrier, inc=1, device_id=sibling, device_id_type=MESH)

    @pl.when(has_above)
    def _():
        pl.semaphore_signal(barrier, inc=1, device_id=above, device_id_type=MESH)

    @pl.when(has_below)
    def _():
        pl.semaphore_signal(barrier, inc=1, device_id=below, device_id_type=MESH)

    for c in range(C):
        wst[c, :, :QW] = wq_ref[:, c * QW:(c + 1) * QW]
        wst[c, :, QW:QW + D] = wkv_ref[:, c * D:(c + 1) * D]
        wst[c, :, QW + D:] = wkv_ref[:, (C + c) * D:(C + c + 1) * D]
    mine = pl.ds(pl.multiple_of(p * T, T), T)
    wbuf[z, k, mine, :] = wst[p]

    pl.semaphore_wait(barrier, C + has_above.astype(jnp.int32) + has_below.astype(jnp.int32))

    def w_copy(d):
        to = lax.rem(p + d, C)
        return copy(wst.at[to], wbuf.at[z, k, mine, :], ws.at[d], wr.at[d], dev(z, to, k))

    def x_copy(d):
        part = xbuf.at[:, mine, :]
        return copy(part, part, xs.at[d], xr.at[d], dev(z, lax.rem(p + d, C), k))

    for d in range(1, C):
        w_copy(d).start()

    @pl.loop(0, T // 16)
    def _(i):
        x = tok_ref[pl.ds(pl.multiple_of(i * 16, 16), 16), :].astype(jnp.float32)
        mean_sq = jnp.mean(x * x, axis=-1, keepdims=True)
        y = (x * lax.rsqrt(mean_sq + 1e-05) * gain_ref[...]).astype(jnp.bfloat16)
        rows = pl.ds(pl.multiple_of(p * T + i * 16, 16), 16)
        for zi in range(Z):
            for ki in range(2):
                for c in range(C):
                    j = ((zi * C + c) * 2 + ki) * T
                    xbuf[zi * 2 + ki, rows, c * T:(c + 1) * T] = y[:, j:j + T]

    for d in range(1, C):
        x_copy(d).start()

    def w_recv(d):
        frm = lax.rem(p + C - d, C)
        slot = wbuf.at[z, k, pl.ds(pl.multiple_of(frm * T, T), T), :]
        copy(slot, slot, ws.at[d], wr.at[d], sibling).wait_recv()

    def x_recv(d):
        frm = lax.rem(p + C - d, C)
        slot = xbuf.at[:, pl.ds(pl.multiple_of(frm * T, T), T), :]
        copy(slot, slot, xs.at[d], xr.at[d], sibling).wait_recv()

    def block_copy(buf, zi, ki, send, recv, device):
        slot = buf.at[zi, ki]
        return copy(slot, slot, send, recv, device)

    def plane_of(zi):
        return lax.rem(zi + Z, Z)

    def up(t):
        return block_copy(wbuf, plane_of(z - t), k, us.at[t], ur.at[t], above)

    def down(t):
        return block_copy(wbuf, plane_of(z + t), k, ds_.at[t], dr.at[t], below)

    def sib(index, zi, ki):
        return block_copy(wbuf, zi, ki, ss.at[index], sr.at[index], sibling)

    for d in range(1, C):
        w_recv(d)

    @pl.when(has_above)
    def _():
        up(0).start()

    @pl.when(has_below)
    def _():
        down(0).start()

    sib(0, z, k).start()

    def step(t):
        @pl.when(z >= t)
        def _():
            block_copy(wbuf, plane_of(z - t), k, us.at[t - 1], ur.at[t - 1], below).wait_recv()

            @pl.when(has_above)
            def _():
                up(t).start()

            sib(t, plane_of(z - t), k).start()

        @pl.when(z + t < Z)
        def _():
            block_copy(wbuf, plane_of(z + t), k, ds_.at[t - 1], dr.at[t - 1], above).wait_recv()

            @pl.when(has_below)
            def _():
                down(t).start()

            sib(Z - 1 + t, plane_of(z + t), k).start()

    def project(zi, index):
        sib(index, zi, 1 - k).wait_recv()

        @pl.loop(0, R // 256)
        def _(i):
            rows = pl.ds(pl.multiple_of(i * 256, 256), 256)
            total = acc[rows, :]
            for ki in range(2):
                total += jnp.dot(
                    xbuf[zi * 2 + ki, rows, :], wbuf[zi, ki],
                    preferred_element_type=jnp.float32,
                )
            acc[rows, :] = total

    def project_step(t):
        @pl.when(z >= t)
        def _():
            project(plane_of(z - t), t)

        @pl.when(z + t < Z)
        def _():
            project(plane_of(z + t), Z - 1 + t)

    acc[...] = jnp.zeros_like(acc)
    for t in range(1, Z - 1):
        step(t)
    for d in range(1, C):
        x_recv(d)
    project(z, 0)
    for t in range(1, Z - 1):
        project_step(t)
    if Z > 1:
        step(Z - 1)
        project_step(Z - 1)

    cos, sin = cos_ref[...], sin_ref[...]

    def rope(u):
        return (u * cos + pltpu.roll(u, D // 2, 1) * sin).astype(jnp.bfloat16)

    kvbuf[z, k, :, :D] = rope(acc[:, QW:QW + D])
    kvbuf[z, k, :, D:] = acc[:, QW + D:].astype(jnp.bfloat16)

    def kv_up(t):
        return block_copy(kvbuf, plane_of(z - t), k, ks.at[t], kr.at[t], above)

    def kv_sib(t, ki):
        return block_copy(kvbuf, plane_of(z - t), ki, kss.at[t], ksr.at[t], sibling)

    kv_sib(0, k).start()

    @pl.when(has_above)
    def _():
        kv_up(0).start()

    for h in range(G):
        qbuf[h] = rope(acc[:, h * D:(h + 1) * D])

    factor = LOG2E / D**0.5
    half = R // 256

    def attend(zi, first):
        @pl.loop(0, G * half)
        def _(i):
            h = i // half
            r0 = pl.multiple_of((i % half) * 256, 256)
            rows = pl.ds(r0, 256)
            q = qbuf[h, rows, :]
            keys = kvbuf[zi, :, :, :D].reshape(2 * R, D)
            vals = kvbuf[zi, :, :, D:].reshape(2 * R, D)
            s = lax.dot_general(
                q, keys, (((1,), (1,)), ((), ())), preferred_element_type=jnp.float32
            )
            if first:
                row = r0 + lax.broadcasted_iota(jnp.int32, (256, 1), 0)
                col = lax.broadcasted_iota(jnp.int32, (1, 2 * R), 1)
                qpos = ((row // T) * 2 + k) * T + row % T
                kpos = (((col % R) // T) * 2 + col // R) * T + col % T
                s = jnp.where(kpos <= qpos, s, -1e30)
                m = jnp.max(s, axis=-1, keepdims=True)
            else:
                old = mbuf[h, rows, :1]
                m = jnp.maximum(old, jnp.max(s, axis=-1, keepdims=True))
            e = jnp.exp2((s - m) * factor)
            total = jnp.sum(e, axis=-1, keepdims=True)
            o = jnp.dot(e.astype(jnp.bfloat16), vals, preferred_element_type=jnp.float32)
            if not first:
                shrink = jnp.exp2((old - m) * factor)
                total += lbuf[h, rows, :1] * shrink
                o += obuf[h, rows, :] * shrink
            mbuf[h, rows, :] = jnp.broadcast_to(m, (256, D))
            lbuf[h, rows, :] = jnp.broadcast_to(total, (256, D))
            obuf[h, rows, :] = o

    def kv_recv(t):
        @pl.when(z >= t)
        def _():
            block_copy(kvbuf, plane_of(z - t), k, ks.at[t - 1], kr.at[t - 1], below).wait_recv()

            @pl.when(has_above)
            def _():
                kv_up(t).start()

            kv_sib(t, k).start()

    kv_sib(0, 1 - k).wait_recv()
    attend(z, True)
    for t in range(1, Z):
        kv_recv(t)

        @pl.when(z >= t)
        def _():
            kv_sib(t, 1 - k).wait_recv()
            attend(plane_of(z - t), False)

    for c in range(C):
        for h in range(G):
            ost[c, :, h * D:(h + 1) * D] = (
                obuf[h, c * T:(c + 1) * T, :] / lbuf[h, c * T:(c + 1) * T, :]
            ).astype(jnp.bfloat16)

    def o_copy(d):
        to = lax.rem(p + d, C)
        return copy(ost.at[to], orecv.at[p], os_.at[d], orr.at[d], dev(z, to, k))

    for d in range(1, C):
        o_copy(d).start()
    orecv[p] = ost[p]
    for d in range(1, C):
        frm = lax.rem(p + C - d, C)
        copy(orecv.at[frm], orecv.at[frm], os_.at[d], orr.at[d], sibling).wait_recv()
    for c in range(C):
        out_ref[:, c * QW:(c + 1) * QW] = orecv[c]

    for d in range(1, C):
        w_copy(d).wait_send()
        x_copy(d).wait_send()
        o_copy(d).wait_send()
    for t in range(Z):
        @pl.when(jnp.logical_and(has_above, z >= t))
        def _():
            up(t).wait_send()
            kv_up(t).wait_send()

        @pl.when(jnp.logical_and(has_below, z + t < Z))
        def _():
            down(t).wait_send()

        @pl.when(z >= t)
        def _():
            sib(t, plane_of(z - t), k).wait_send()
            kv_sib(t, k).wait_send()

        if t > 0:
            @pl.when(z + t < Z)
            def _():
                sib(Z - 1 + t, plane_of(z + t), k).wait_send()


def on_device(planes, tokens, gain, w_query, key_value_weight):
    T, M = tokens.shape
    D = HEAD_WIDTH
    C = key_value_weight.shape[1] // (2 * D)
    G = HQ // C
    R = C * T
    Z = planes
    width = (G + 2) * D
    me = lax.axis_index("seq")
    first = (me // (2 * C)) * (2 * C) + me % 2
    row = jnp.arange(R, dtype=jnp.int32)
    positions = (first + (row // T) * 2) * T + row % T
    lane = jnp.arange(D, dtype=jnp.int32)
    half = (lane % (D // 2)).astype(jnp.float32)
    frequency = ROPE_BASE ** (-(half * 2.0 / D))
    angles = positions.astype(jnp.float32)[:, None] * frequency[None, :]
    cos = jnp.cos(angles)
    sin = jnp.where(lane < D // 2, -1.0, 1.0)[None, :] * jnp.sin(angles)
    bf, f32 = jnp.bfloat16, jnp.float32
    sem = pltpu.SemaphoreType.DMA
    vm = pl.BlockSpec(memory_space=pltpu.VMEM)
    return pl.pallas_call(
        functools.partial(kernel, Z, C),
        out_shape=jax.ShapeDtypeStruct((T, HQ * D), bf),
        in_specs=[vm] * 6,
        out_specs=vm,
        scratch_shapes=[
            pltpu.VMEM((C, T, width), bf),
            pltpu.VMEM((Z, 2, R, width), bf),
            pltpu.VMEM((2 * Z, R, M // (2 * Z)), bf),
            pltpu.VMEM((R, width), f32),
            pltpu.VMEM((G, R, D), bf),
            pltpu.VMEM((Z, 2, R, 2 * D), bf),
            pltpu.VMEM((G, R, D), f32),
            pltpu.VMEM((G, R, D), f32),
            pltpu.VMEM((G, R, D), f32),
            pltpu.VMEM((C, T, G * D), bf),
            pltpu.VMEM((C, T, G * D), bf),
            sem((C,)), sem((C,)), sem((C,)), sem((C,)),
            sem((Z,)), sem((Z,)), sem((Z,)), sem((Z,)),
            sem((2 * Z,)), sem((2 * Z,)),
            sem((Z,)), sem((Z,)), sem((Z,)), sem((Z,)),
            sem((C,)), sem((C,)),
        ],
        compiler_params=pltpu.CompilerParams(
            collective_id=0, has_side_effects=True, vmem_limit_bytes=48 * 1024 * 1024
        ),
    )(tokens, gain[None, :], w_query, key_value_weight, cos, sin)


def solution(mesh):
    return jax.shard_map(
        lambda a, b, c, d: on_device(
            mesh.shape["seq"] // (2 * (d.shape[1] // (2 * HEAD_WIDTH))), a, b, c, d
        ),
        mesh=mesh,
        in_specs=(P(("grp", "seq"), None), P(), P("seq", None), P("seq", None)),
        out_specs=P(("grp", "seq"), None),
        check_vma=False,
    )
```

```python
import functools

import jax
import jax.numpy as jnp
from jax import lax
from jax.experimental import pallas as pl
from jax.experimental.pallas import tpu as pltpu
from jax.sharding import PartitionSpec as P

HEAD_WIDTH = 128
HQ = 16
ROPE_BASE = 500000.0
LOG2E = 1.4426950408889634
MESH = pl.DeviceIdType.MESH


def kernel(
    planes, kv_heads, tok_ref, gain_ref, wq_ref, wkv_ref, cos_ref, sin_ref, out_ref,
    kvst, qst, kvw, qw, xbuf, kacc, qacc, qbuf, kvbuf, mbuf, lbuf, obuf, ost, orecv,
    kw_s, kw_r, ku_s, ku_r, kd_s, kd_r, kb_s, kb_r,
    qw_s, qw_r, qu_s, qu_r, qd_s, qd_r, qb_s, qb_r,
    xs, xr, ks, kr, kss, ksr, os_, orr,
):
    C, Z, D = kv_heads, planes, HEAD_WIDTH
    T, M = tok_ref.shape
    G = HQ // C
    QW = G * D
    R = C * T
    me = lax.axis_index("seq")
    z = me // (2 * C)
    p = (me % (2 * C)) // 2
    k = me % 2

    def dev(zi, pi, ki):
        return {"seq": (zi * C + pi) * 2 + ki}

    sibling = dev(z, p, 1 - k)
    above = dev(lax.rem(z + 1, Z), p, k)
    below = dev(lax.rem(z + Z - 1, Z), p, k)
    has_above = z < Z - 1
    has_below = z > 0

    def copy(src, dst, send, recv, device):
        return pltpu.make_async_remote_copy(
            src_ref=src, dst_ref=dst, send_sem=send, recv_sem=recv,
            device_id=device, device_id_type=MESH,
        )

    def rows_of(owner):
        return pl.ds(pl.multiple_of(owner * T, T), T)

    barrier = pltpu.get_barrier_semaphore()
    for d in range(1, C):
        pl.semaphore_signal(barrier, inc=1, device_id=dev(z, lax.rem(p + d, C), k), device_id_type=MESH)
    pl.semaphore_signal(barrier, inc=1, device_id=sibling, device_id_type=MESH)

    @pl.when(has_above)
    def _():
        pl.semaphore_signal(barrier, inc=1, device_id=above, device_id_type=MESH)

    @pl.when(has_below)
    def _():
        pl.semaphore_signal(barrier, inc=1, device_id=below, device_id_type=MESH)

    kv_w = (kvst, kvw, kw_s, kw_r, ku_s, ku_r, kd_s, kd_r, kb_s, kb_r)
    q_w = (qst, qw, qw_s, qw_r, qu_s, qu_r, qd_s, qd_r, qb_s, qb_r)

    for c in range(C):
        kvst[c, :, :D] = wkv_ref[:, c * D:(c + 1) * D]
        kvst[c, :, D:] = wkv_ref[:, (C + c) * D:(C + c + 1) * D]
        qst[c] = wq_ref[:, c * QW:(c + 1) * QW]
    kvw[z, k, rows_of(p), :] = kvst[p]
    qw[z, k, rows_of(p), :] = qst[p]

    pl.semaphore_wait(barrier, C + has_above.astype(jnp.int32) + has_below.astype(jnp.int32))

    def plane_of(zi):
        return lax.rem(zi + Z, Z)

    def w_copy(w, d):
        to = lax.rem(p + d, C)
        return copy(w[0].at[to], w[1].at[z, k, rows_of(p), :], w[2].at[d], w[3].at[d], dev(z, to, k))

    def piece(w, d, s, device, ki=None, zi=None):
        frm = lax.rem(p + C - d, C)
        slot = w[1].at[z if zi is None else zi, k if ki is None else ki, rows_of(frm), :]
        return copy(slot, slot, w[s].at[d], w[s + 1].at[d], device)

    def block(w, zi, index, s, device, ki=None):
        slot = w[1].at[zi, k if ki is None else ki]
        return copy(slot, slot, w[s].at[C - 1 + index], w[s + 1].at[C - 1 + index], device)

    def send_piece(w, d):
        @pl.when(has_above)
        def _():
            piece(w, d, 4, above).start()

        @pl.when(has_below)
        def _():
            piece(w, d, 6, below).start()

        piece(w, d, 8, sibling).start()

    def first_step(w):
        for d in range(1, C):
            piece(w, d, 2, sibling).wait_recv()
            send_piece(w, d)

    def step(w, t):
        @pl.when(z >= t)
        def _():
            zi = plane_of(z - t)
            if t == 1:
                for d in range(C):
                    piece(w, d, 4, below, zi=zi).wait_recv()
            else:
                block(w, zi, t - 1, 4, below).wait_recv()

            @pl.when(has_above)
            def _():
                block(w, zi, t, 4, above).start()

            block(w, zi, t, 8, sibling).start()

        @pl.when(z + t < Z)
        def _():
            zi = plane_of(z + t)
            if t == 1:
                for d in range(C):
                    piece(w, d, 6, above, zi=zi).wait_recv()
            else:
                block(w, zi, t - 1, 6, above).wait_recv()

            @pl.when(has_below)
            def _():
                block(w, zi, t, 6, below).start()

            block(w, zi, Z - 1 + t, 8, sibling).start()

    def project(w, acc, zi):
        @pl.loop(0, R // 256)
        def _(i):
            rows = pl.ds(pl.multiple_of(i * 256, 256), 256)
            total = acc[rows, :]
            for ki in range(2):
                total += jnp.dot(
                    xbuf[zi * 2 + ki, rows, :], w[1][zi, ki],
                    preferred_element_type=jnp.float32,
                )
            acc[rows, :] = total

    def project_step(w, acc, t):
        if t == 0:
            for d in range(C):
                piece(w, d, 8, sibling, ki=1 - k).wait_recv()
            project(w, acc, z)
            return

        @pl.when(z >= t)
        def _():
            zi = plane_of(z - t)
            block(w, zi, t, 8, sibling, ki=1 - k).wait_recv()
            project(w, acc, zi)

        @pl.when(z + t < Z)
        def _():
            zi = plane_of(z + t)
            block(w, zi, Z - 1 + t, 8, sibling, ki=1 - k).wait_recv()
            project(w, acc, zi)

    def x_part(owner, half):
        return xbuf.at[:, pl.ds(pl.multiple_of(owner * T + half * (T // 2), T // 2), T // 2), :]

    peers = (p + 1 - 2 * lax.rem(p, 2), lax.rem(p + 2, 4))
    far = 3 - p

    def x_copy(peer, half, owner, index):
        part = x_part(owner, half)
        return copy(part, part, xs.at[index], xr.at[index], dev(z, peers[peer], k))

    def x_out(index):
        if index < 4:
            return x_copy(index // 2, index % 2, p, index)
        return x_copy(5 - index, index - 4, peers[index - 4], index)

    def x_in(index):
        if index < 4:
            return x_copy(index // 2, index % 2, peers[index // 2], index)
        return x_copy(5 - index, index - 4, far, index)

    for d in range(1, C):
        w_copy(kv_w, d).start()
    send_piece(kv_w, 0)
    for d in range(1, C):
        w_copy(q_w, d).start()
    send_piece(q_w, 0)

    @pl.loop(0, T // 16)
    def _(i):
        x = tok_ref[pl.ds(pl.multiple_of(i * 16, 16), 16), :].astype(jnp.float32)
        mean_sq = jnp.mean(x * x, axis=-1, keepdims=True)
        y = (x * lax.rsqrt(mean_sq + 1e-05) * gain_ref[...]).astype(jnp.bfloat16)
        rows = pl.ds(pl.multiple_of(p * T + i * 16, 16), 16)
        for zi in range(Z):
            for ki in range(2):
                for c in range(C):
                    j = ((zi * C + c) * 2 + ki) * T
                    xbuf[zi * 2 + ki, rows, c * T:(c + 1) * T] = y[:, j:j + T]

    for index in (0, 3, 1, 2):
        x_out(index).start()

    def forward_x():
        x_in(0).wait_recv()
        x_out(4).start()
        x_in(3).wait_recv()
        x_out(5).start()

    first_step(kv_w)
    first_step(q_w)
    kacc[...] = jnp.zeros_like(kacc)
    qacc[...] = jnp.zeros_like(qacc)
    for t in range(1, Z - 1):
        step(kv_w, t)
        step(q_w, t)
        if t == 1:
            forward_x()
    if Z < 3:
        forward_x()
    if Z > 1:
        step(kv_w, Z - 1)
    for index in (1, 2, 4, 5):
        x_in(index).wait_recv()
    for t in range(Z):
        project_step(kv_w, kacc, t)

    cos, sin = cos_ref[...], sin_ref[...]

    def rope(u):
        return (u * cos + pltpu.roll(u, D // 2, 1) * sin).astype(jnp.bfloat16)

    kvbuf[z, k, :, :D] = rope(kacc[:, :D])
    kvbuf[z, k, :, D:] = kacc[:, D:].astype(jnp.bfloat16)

    def block_copy(buf, zi, ki, send, recv, device):
        slot = buf.at[zi, ki]
        return copy(slot, slot, send, recv, device)

    def kv_up(t):
        return block_copy(kvbuf, plane_of(z - t), k, ks.at[t], kr.at[t], above)

    def kv_sib(t, ki):
        return block_copy(kvbuf, plane_of(z - t), ki, kss.at[t], ksr.at[t], sibling)

    kv_sib(0, k).start()

    @pl.when(has_above)
    def _():
        kv_up(0).start()

    def kv_recv(t):
        @pl.when(z >= t)
        def _():
            block_copy(kvbuf, plane_of(z - t), k, ks.at[t - 1], kr.at[t - 1], below).wait_recv()

            @pl.when(has_above)
            def _():
                kv_up(t).start()

            kv_sib(t, k).start()

    if Z > 1:
        kv_recv(1)
    for t in range(Z - 1):
        project_step(q_w, qacc, t)
    if Z > 1:
        step(q_w, Z - 1)
    if Z > 2:
        kv_recv(2)
    if Z > 1:
        project_step(q_w, qacc, Z - 1)
    else:
        project_step(q_w, qacc, 0)

    for h in range(G):
        qbuf[h] = rope(qacc[:, h * D:(h + 1) * D])

    factor = LOG2E / D**0.5
    half = R // 256

    def attend(zi, first):
        @pl.loop(0, G * half)
        def _(i):
            h = i // half
            r0 = pl.multiple_of((i % half) * 256, 256)
            rows = pl.ds(r0, 256)
            q = qbuf[h, rows, :]
            keys = kvbuf[zi, :, :, :D].reshape(2 * R, D)
            vals = kvbuf[zi, :, :, D:].reshape(2 * R, D)
            s = lax.dot_general(
                q, keys, (((1,), (1,)), ((), ())), preferred_element_type=jnp.float32
            )
            if first:
                row = r0 + lax.broadcasted_iota(jnp.int32, (256, 1), 0)
                col = lax.broadcasted_iota(jnp.int32, (1, 2 * R), 1)
                qpos = ((row // T) * 2 + k) * T + row % T
                kpos = (((col % R) // T) * 2 + col // R) * T + col % T
                s = jnp.where(kpos <= qpos, s, -1e30)
                m = jnp.max(s, axis=-1, keepdims=True)
            else:
                old = mbuf[h, rows, :1]
                m = jnp.maximum(old, jnp.max(s, axis=-1, keepdims=True))
            e = jnp.exp2((s - m) * factor)
            total = jnp.sum(e, axis=-1, keepdims=True)
            o = jnp.dot(e.astype(jnp.bfloat16), vals, preferred_element_type=jnp.float32)
            if not first:
                shrink = jnp.exp2((old - m) * factor)
                total += lbuf[h, rows, :1] * shrink
                o += obuf[h, rows, :] * shrink
            mbuf[h, rows, :] = jnp.broadcast_to(m, (256, D))
            lbuf[h, rows, :] = jnp.broadcast_to(total, (256, D))
            obuf[h, rows, :] = o

    kv_sib(0, 1 - k).wait_recv()
    attend(z, True)
    for t in range(1, Z):
        if t > 2:
            kv_recv(t)

        @pl.when(z >= t)
        def _():
            kv_sib(t, 1 - k).wait_recv()
            attend(plane_of(z - t), False)

    for c in range(C):
        for h in range(G):
            ost[c, :, h * D:(h + 1) * D] = (
                obuf[h, c * T:(c + 1) * T, :] / lbuf[h, c * T:(c + 1) * T, :]
            ).astype(jnp.bfloat16)

    def o_copy(d):
        to = lax.rem(p + d, C)
        return copy(ost.at[to], orecv.at[p], os_.at[d], orr.at[d], dev(z, to, k))

    for d in range(1, C):
        o_copy(d).start()
    orecv[p] = ost[p]
    for d in range(1, C):
        frm = lax.rem(p + C - d, C)
        copy(orecv.at[frm], orecv.at[frm], os_.at[d], orr.at[d], sibling).wait_recv()
    for c in range(C):
        out_ref[:, c * QW:(c + 1) * QW] = orecv[c]

    for d in range(1, C):
        o_copy(d).wait_send()
    for index in range(6):
        x_out(index).wait_send()
    for w in (kv_w, q_w):
        for d in range(C):
            if d > 0:
                w_copy(w, d).wait_send()

            @pl.when(has_above)
            def _():
                piece(w, d, 4, above).wait_send()

            @pl.when(has_below)
            def _():
                piece(w, d, 6, below).wait_send()

            piece(w, d, 8, sibling).wait_send()
        for t in range(1, Z):
            @pl.when(jnp.logical_and(has_above, z >= t))
            def _():
                block(w, plane_of(z - t), t, 4, above).wait_send()

            @pl.when(jnp.logical_and(has_below, z + t < Z))
            def _():
                block(w, plane_of(z + t), t, 6, below).wait_send()

            @pl.when(z >= t)
            def _():
                block(w, plane_of(z - t), t, 8, sibling).wait_send()

            @pl.when(z + t < Z)
            def _():
                block(w, plane_of(z + t), Z - 1 + t, 8, sibling).wait_send()
    for t in range(Z):
        @pl.when(jnp.logical_and(has_above, z >= t))
        def _():
            kv_up(t).wait_send()

        @pl.when(z >= t)
        def _():
            kv_sib(t, k).wait_send()


def on_device(planes, tokens, gain, w_query, key_value_weight):
    T, M = tokens.shape
    D = HEAD_WIDTH
    C = key_value_weight.shape[1] // (2 * D)
    G = HQ // C
    R = C * T
    Z = planes
    me = lax.axis_index("seq")
    first = (me // (2 * C)) * (2 * C) + me % 2
    row = jnp.arange(R, dtype=jnp.int32)
    positions = (first + (row // T) * 2) * T + row % T
    lane = jnp.arange(D, dtype=jnp.int32)
    half = (lane % (D // 2)).astype(jnp.float32)
    frequency = ROPE_BASE ** (-(half * 2.0 / D))
    angles = positions.astype(jnp.float32)[:, None] * frequency[None, :]
    cos = jnp.cos(angles)
    sin = jnp.where(lane < D // 2, -1.0, 1.0)[None, :] * jnp.sin(angles)
    bf, f32 = jnp.bfloat16, jnp.float32
    sem = pltpu.SemaphoreType.DMA
    vm = pl.BlockSpec(memory_space=pltpu.VMEM)
    return pl.pallas_call(
        functools.partial(kernel, Z, C),
        out_shape=jax.ShapeDtypeStruct((T, HQ * D), bf),
        in_specs=[vm] * 6,
        out_specs=vm,
        scratch_shapes=[
            pltpu.VMEM((C, T, 2 * D), bf),
            pltpu.VMEM((C, T, G * D), bf),
            pltpu.VMEM((Z, 2, R, 2 * D), bf),
            pltpu.VMEM((Z, 2, R, G * D), bf),
            pltpu.VMEM((2 * Z, R, M // (2 * Z)), bf),
            pltpu.VMEM((R, 2 * D), f32),
            pltpu.VMEM((R, G * D), f32),
            pltpu.VMEM((G, R, D), bf),
            pltpu.VMEM((Z, 2, R, 2 * D), bf),
            pltpu.VMEM((G, R, D), f32),
            pltpu.VMEM((G, R, D), f32),
            pltpu.VMEM((G, R, D), f32),
            pltpu.VMEM((C, T, G * D), bf),
            pltpu.VMEM((C, T, G * D), bf),
            sem((C,)), sem((C,)), sem((C + Z,)), sem((C + Z,)),
            sem((C + Z,)), sem((C + Z,)), sem((C + 2 * Z,)), sem((C + 2 * Z,)),
            sem((C,)), sem((C,)), sem((C + Z,)), sem((C + Z,)),
            sem((C + Z,)), sem((C + Z,)), sem((C + 2 * Z,)), sem((C + 2 * Z,)),
            sem((6,)), sem((6,)),
            sem((Z,)), sem((Z,)), sem((Z,)), sem((Z,)),
            sem((C,)), sem((C,)),
        ],
        compiler_params=pltpu.CompilerParams(
            collective_id=0, has_side_effects=True, vmem_limit_bytes=48 * 1024 * 1024
        ),
    )(tokens, gain[None, :], w_query, key_value_weight, cos, sin)


def solution(mesh):
    return jax.shard_map(
        lambda a, b, c, d: on_device(
            mesh.shape["seq"] // (2 * (d.shape[1] // (2 * HEAD_WIDTH))), a, b, c, d
        ),
        mesh=mesh,
        in_specs=(P(("grp", "seq"), None), P(), P("seq", None), P("seq", None)),
        out_specs=P(("grp", "seq"), None),
        check_vma=False,
    )
```
